32 devices in a mesh: seq: 8 (over z, x), head: 4 (over y, core).
Axes of the slice: x: 2, y: 2, z: 4, core: 2. Of those that a mesh axis runs over, the one named last changes fastest.
Arguments:
- queries: bfloat16 [1024, 8192], P('seq', 'head'), may hold values from -6 to 6
- memory_keys: bfloat16 [1024, 8192], P('seq', 'head'), may hold values from -6 to 6
- memory_values: bfloat16 [1024, 8192], P('seq', 'head'), may hold values from -6 to 6
- log_decay: float32 [1024, 64], P('seq', 'head'), may hold values from -3 to 0, as said below
- hidden_in: int32 [1024, 6144], P('seq', 'head'), may hold values from -127 to 127
- out_weight: bfloat16 [8192, 6144], P('head'), may hold values from -1 to 1, as said below
- routes: int32 [1024, 2], P('seq'), may hold values from 0 to 3, all different within a row; in each aligned block of 128 rows (0 to 127, 128 to 255, ...) at most 80 rows name the same one
- route_weight: float32 [1024, 2], P('seq'), may hold values from 0.25 to 1
- gate_weight: bfloat16 [6144, 36864], P(None, ('seq', 'head')), may hold values from -1 to 1, as said below
- up_weight: bfloat16 [6144, 36864], P(None, ('seq', 'head')), may hold values from -1 to 1, as said below
- down_weight: bfloat16 [36864, 6144], P(('seq', 'head')), may hold values from -1 to 1, as said below
- scales: float32 [14], replicated, may hold values from 0.5 to 2
Outputs:
- layer_out: bfloat16 [1024, 6144], P('seq', 'head')
The draws below stay inside these ranges and needn't reach their ends.
Inputs may be any that keep to these rules, and one draw needn't show every extreme that they name: `routes`: each row names two different experts; among the rows of one device no expert is named by more than 80 rows. `log_decay`: every entry is negative. `out_weight`: every entry is -1, 0 or 1. `gate_weight`: every entry is -1, 0 or 1. `up_weight`: every entry is -1, 0 or 1. `down_weight`: every entry is -1, 0 or 1.
All inputs are finite; a program needn't handle non-finite values.
Results may differ from the reference program's by a relative error of at most 0.02.
Values may be sent and summed in bfloat16 or wider, within the bound.
A program may use at most 128 MiB of HBM per device.

```python
import math
import jax
import jax.numpy as jnp
import numpy as np
from jax import lax

D = 6144
FF = 9216
HEADS = 64
HEAD_DIM = 128
EXPERTS = 4
TOK_DEV = 128
SPAN_OF_STEPS = 1024
CAP = 80
SLICE = 1152
N_SEQ = 8


def ternary(key, shape, salt):
    base = jax.random.fold_in(key, salt)
    signs = jax.random.randint(jax.random.fold_in(base, 1), shape, -1, 2)
    return signs.astype(jnp.float32).astype(jnp.bfloat16)


def draw_out_weight(key, part):
    return ternary(key, (HEADS * HEAD_DIM, D), 11)


def draw_gate_weight(key, part):
    return ternary(key, (D, EXPERTS * FF), 12)


def draw_up_weight(key, part):
    return ternary(key, (D, EXPERTS * FF), 13)


def draw_down_weight(key, part):
    return ternary(key, (EXPERTS * FF, D), 14)


def draw_hidden_in(key, part):
    base = jax.random.fold_in(key, 21)
    column = jnp.arange(D, dtype=jnp.int32)
    reach = 4 + 123 * column // (D - 1)
    return jax.random.randint(base, (SPAN_OF_STEPS, D), -reach[None, :], reach[None, :] + 1).astype(jnp.int32)


def draw_log_decay(key, part):
    base = jax.random.fold_in(key, 31)
    arriving_streams = [jax.random.fold_in(base, index) for index in range(8)]
    share = 0.5
    slow = jax.random.uniform(arriving_streams[0], (HEADS,)) < share
    slow_rate = jnp.exp(jax.random.uniform(arriving_streams[1], (HEADS,), minval=math.log(0.1), maxval=math.log(0.4))) / SPAN_OF_STEPS
    fast_rate = jnp.exp(jax.random.uniform(arriving_streams[2], (HEADS,), minval=0.0, maxval=math.log(4.0))) / TOK_DEV
    fading_factors = jnp.where(slow, slow_rate, fast_rate)
    device_factor = jnp.exp(jax.random.uniform(arriving_streams[3], (N_SEQ, 1, HEADS), minval=math.log(0.5), maxval=math.log(1.5)))
    jitter = jax.random.uniform(arriving_streams[4], (N_SEQ, TOK_DEV, HEADS), minval=0.5, maxval=1.5)
    fading_factors = (fading_factors[None, None, :] * device_factor * jitter).reshape(SPAN_OF_STEPS, HEADS)
    packet_clusters = jax.random.randint(arriving_streams[5], (2,), 0, SPAN_OF_STEPS)
    objective_scores = jax.random.uniform(arriving_streams[6], (2, HEADS), minval=0.22, maxval=0.6)
    fading_factors = fading_factors.at[packet_clusters].add(objective_scores)
    return (-fading_factors).astype(jnp.float32)


def block_levels(own_key, dims, cuts, low, high):
    def one(axis_at, parts):
        heights = jax.random.uniform(jax.random.fold_in(jax.random.fold_in(own_key, 6), axis_at), (parts,), jnp.float32, low / len(cuts), high / len(cuts))
        return jnp.repeat(jnp.exp(heights), dims[axis_at] // parts).reshape((-1,) + (1,) * (len(dims) - axis_at - 1))

    factor_of = one(*cuts[0])
    for cut in cuts[1:]:
        factor_of = factor_of * one(*cut)
    return factor_of


def routed_block(rng, own, number, rows, count, top, bound, slope):
    order = jax.random.permutation(rng, count)
    crowded, common = load_shares(count, rows * top, bound, slope, True), load_shares(count, rows * top, bound, slope, False)
    places = jnp.arange(count)

    def named(sizes, rotation):
        used = int((sizes > 0).sum())
        fixed = max(1, used // 4)
        shifted = fixed + (places - fixed + rotation * (used - fixed)) % max(1, count - fixed)
        return jnp.zeros((count,), jnp.int32).at[order[jnp.where(places < fixed, places, shifted)]].set(jnp.asarray(sizes, jnp.int32))

    sizes = jnp.where(number % 4 == 0, named(crowded, number // 4), named(common, number - number // 4 - 1))
    mixed = jax.random.permutation(jax.random.fold_in(own, 3), count)
    donor, sink = mixed[0:count // 2 * 2:2], mixed[1:count // 2 * 2:2]
    slack = jnp.minimum(sizes[donor] - 1, bound - sizes[sink]) // 2
    slack = jnp.where((donor == order[0]) | (sink == order[0]) | (sizes[sink] == 0), 0, jnp.maximum(slack, 0))
    shifted = jax.random.randint(jax.random.fold_in(own, 4), (count // 2,), 0, 1 << 20) % (slack + 1)
    sizes = sizes.at[donor].add(-shifted).at[sink].add(shifted)
    items = jnp.searchsorted(jnp.cumsum(sizes), jnp.arange(rows * top), side="right").astype(jnp.int32)
    listing = items.reshape(top, rows).T
    listing = listing[jax.random.permutation(jax.random.fold_in(own, 1), rows)]
    rotation = jax.random.randint(jax.random.fold_in(own, 2), (rows, 1), 0, top)
    return jnp.take_along_axis(listing, (jnp.arange(top)[None, :] + rotation) % top, axis=1)


def load_shares(amount, total, most, lean, full):
    portions = [(1 << 20) // math.isqrt(grade ** lean) + 1 for grade in range(1, amount + 1)]
    largest = most if full else min(most, max(-(-total // amount), total * portions[0] // sum(portions)))
    least = 1 if total - largest >= amount - 1 else 0
    holding, surplus = [largest] + [least] * (amount - 1), total - largest - least * (amount - 1)
    while surplus > 0:
        movable = [i for i in range(1, amount) if holding[i] < largest] or [i for i in range(1, amount) if holding[i] < most]
        whole, remaining = sum([portions[i] for i in movable]), surplus
        for i in movable:
            extra = min(most - holding[i], max(1, remaining * portions[i] // whole), surplus)
            holding[i] = holding[i] + extra
            surplus = surplus - extra
    return np.array(holding)


def gaussian(own_key, dims, deviation, most, pieces=(), held_as=jnp.bfloat16):
    factor_of = block_levels(own_key, dims, pieces, -0.22, 0.18) if pieces else 1.0
    drawn = jax.random.normal(own_key, dims, jnp.float32) * deviation * factor_of
    return jnp.minimum(jnp.maximum(drawn, -most), most).astype(held_as)


def setup_inputs(seed: int = 0) -> dict:
    key_list = jax.random.split(jax.random.key(seed), 13)
    queries = gaussian(key_list[0], (SPAN_OF_STEPS, HEADS * HEAD_DIM), 1.0, 6.0, ((0, 8), (1, 4)))
    memory_keys = gaussian(key_list[1], (SPAN_OF_STEPS, HEADS * HEAD_DIM), 1.0, 6.0, ((0, 8), (1, 4)))
    memory_values = gaussian(key_list[2], (SPAN_OF_STEPS, HEADS * HEAD_DIM), 1.0, 6.0, ((0, 8), (1, 4)))
    log_decay = draw_log_decay(jax.random.fold_in(key_list[12], 71), 0)
    hidden_in = draw_hidden_in(jax.random.fold_in(key_list[12], 71), 0)
    out_weight = draw_out_weight(jax.random.fold_in(key_list[12], 71), 0)
    routes_keys = jax.random.split(jax.random.fold_in(key_list[6], 1), SPAN_OF_STEPS // TOK_DEV)
    routes_turns = jax.random.permutation(jax.random.fold_in(key_list[6], 3), SPAN_OF_STEPS // TOK_DEV)
    routes = jax.vmap(lambda own, number: routed_block(jax.random.fold_in(key_list[6], 2), own, number, TOK_DEV, EXPERTS, 2, CAP, 2))(routes_keys, routes_turns).reshape((SPAN_OF_STEPS, 2))
    route_weight = jnp.clip(0.25 + 0.75 * jax.random.uniform(key_list[7], (SPAN_OF_STEPS, 2), jnp.float32) ** block_levels(key_list[7], (SPAN_OF_STEPS, 2), ((0, 8),), -0.2, 0.2), 0.25, 1.0)
    gate_weight = draw_gate_weight(jax.random.fold_in(key_list[12], 71), 0)
    up_weight = draw_up_weight(jax.random.fold_in(key_list[12], 71), 0)
    down_weight = draw_down_weight(jax.random.fold_in(key_list[12], 71), 0)
    scales = jnp.clip(jnp.exp(jax.random.uniform(key_list[11], (2 + 3 * EXPERTS,), jnp.float32, math.log(0.5), math.log(2.0))), 0.5, 2.0)
    return {"queries": queries, "memory_keys": memory_keys, "memory_values": memory_values, "log_decay": log_decay, "hidden_in": hidden_in, "out_weight": out_weight, "routes": routes, "route_weight": route_weight, "gate_weight": gate_weight, "up_weight": up_weight, "down_weight": down_weight, "scales": scales}


def attend_blocks(queries, memory_keys, memory_values, log_decay):
    query_blocks = queries.astype(jnp.float32).reshape(N_SEQ, TOK_DEV, HEADS, HEAD_DIM)
    key_blocks = memory_keys.astype(jnp.float32).reshape(N_SEQ, TOK_DEV, HEADS, HEAD_DIM)
    value_blocks = memory_values.astype(jnp.float32).reshape(N_SEQ, TOK_DEV, HEADS, HEAD_DIM)
    cumulative = jnp.cumsum(log_decay, axis=0)
    block_cum = cumulative.reshape(N_SEQ, TOK_DEV, HEADS)
    ends = block_cum[:, TOK_DEV - 1, :]
    starts = jnp.concatenate([jnp.zeros((1, HEADS), jnp.float32), ends[:-1]], axis=0)
    causal = jnp.arange(TOK_DEV)[:, None] >= jnp.arange(TOK_DEV)[None, :]

    def one_block(carried, inputs):
        query_block, key_block, value_block, cum_block, start, end = inputs
        scores = jnp.einsum('thd,shd->hts', query_block, key_block)
        spread = cum_block.T[:, :, None] - cum_block.T[:, None, :]
        weights = jnp.where(causal[None], scores * jnp.exp(jnp.minimum(spread, 0.0)), 0.0).astype(jnp.bfloat16)
        weights = lax.optimization_barrier(weights).astype(jnp.float32)
        inside = jnp.einsum('hts,shd->thd', weights, value_block)
        lifted = query_block * jnp.exp(cum_block - start[None, :])[:, :, None]
        across = jnp.einsum('thd,hde->the', lifted, carried, precision=lax.Precision.HIGHEST)
        decayed = (key_block * jnp.exp(end[None, :] - cum_block)[:, :, None]).astype(jnp.bfloat16)
        decayed = lax.optimization_barrier(decayed).astype(jnp.float32)
        state = jnp.einsum('shd,she->hde', decayed, value_block)
        carried = jnp.exp(end - start)[:, None, None] * carried + state
        return (carried, inside + across)
    initial = jnp.zeros((HEADS, HEAD_DIM, HEAD_DIM), jnp.float32)
    unused, outputs = lax.scan(one_block, initial, (query_blocks, key_blocks, value_blocks, block_cum, starts, ends))
    return outputs.reshape(SPAN_OF_STEPS, HEADS, HEAD_DIM)

def experts_out(normed, routes, route_weight, gate_weight, up_weight, down_weight, scales):
    padded = jnp.concatenate([normed, jnp.zeros((1, D), jnp.bfloat16)], axis=0)
    order = jnp.arange(SPAN_OF_STEPS, dtype=jnp.int32)
    slots = N_SEQ * CAP

    def one_expert(moe, expert):
        hits = jnp.any(routes == expert, axis=1)
        places = jnp.cumsum(hits.astype(jnp.int32), dtype=jnp.int32) - 1
        target = jnp.where(hits, places, slots).astype(jnp.int32)
        table = jnp.full((slots,), SPAN_OF_STEPS, jnp.int32).at[target].set(order, mode='drop')
        rows = padded[table]
        gate_cols = lax.dynamic_slice_in_dim(gate_weight, (expert * FF).astype(jnp.int32), FF, 1)
        up_cols = lax.dynamic_slice_in_dim(up_weight, (expert * FF).astype(jnp.int32), FF, 1)
        gate = jnp.dot(rows, gate_cols, preferred_element_type=jnp.float32) * (scales[2 + expert] * D ** (-0.5))
        up = jnp.dot(rows, up_cols, preferred_element_type=jnp.float32) * (scales[2 + EXPERTS + expert] * D ** (-0.5))
        act = (jax.nn.silu(gate) * up).astype(jnp.bfloat16)
        down_scale = scales[2 + 2 * EXPERTS + expert] * FF ** (-0.5)

        def one_slice(total, index):
            piece = lax.dynamic_slice_in_dim(act, (index * SLICE).astype(jnp.int32), SLICE, 1)
            down_rows = lax.dynamic_slice_in_dim(down_weight, (expert * FF + index * SLICE).astype(jnp.int32), SLICE, 0)
            part = (jnp.dot(piece, down_rows, preferred_element_type=jnp.float32) * down_scale).astype(jnp.bfloat16)
            return (total + lax.optimization_barrier(part).astype(jnp.float32), None)
        summed, unused = lax.scan(one_slice, jnp.zeros((slots, D), jnp.float32), jnp.arange(FF // SLICE, dtype=jnp.int32))
        weight = lax.optimization_barrier(jnp.sum(jnp.where(routes == expert, route_weight, 0.0), axis=1))
        picked = summed[jnp.clip(places, 0, slots - 1)]
        return (moe + jnp.where(hits[:, None], weight[:, None] * picked, 0.0), None)
    moe, unused = lax.scan(one_expert, jnp.zeros((SPAN_OF_STEPS, D), jnp.float32), jnp.arange(EXPERTS, dtype=jnp.int32))
    return moe

def reference(queries, memory_keys, memory_values, log_decay, hidden_in, out_weight, routes, route_weight, gate_weight, up_weight, down_weight, scales):
    mixer_output = attend_blocks(queries, memory_keys, memory_values, log_decay)
    heads_out = (mixer_output * lax.rsqrt(lax.optimization_barrier(jnp.mean(mixer_output * mixer_output, axis=2, keepdims=True)) + 1e-06)).astype(jnp.bfloat16)
    heads_out = heads_out.reshape(SPAN_OF_STEPS, HEADS * HEAD_DIM)
    attention = jnp.dot(heads_out, out_weight, preferred_element_type=jnp.float32) * (scales[1] * 0.5 * (HEADS * HEAD_DIM) ** (-0.5))
    resid = scales[0] / 64.0 * hidden_in.astype(jnp.float32) + attention
    normed = (resid * lax.rsqrt(lax.optimization_barrier(jnp.mean(resid * resid, axis=1, keepdims=True)) + 1e-05)).astype(jnp.bfloat16)
    moe = experts_out(normed, routes, route_weight, gate_weight, up_weight, down_weight, scales)
    return (resid + moe).astype(jnp.bfloat16)
```

```python
import functools

import jax
import jax.numpy as jnp
from jax import lax
from jax.experimental import pallas as pl
from jax.experimental.pallas import tpu as pltpu
from jax.sharding import PartitionSpec as P

D = 6144
FF = 9216
HEADS = 64
HEAD_DIM = 128
EXPERTS = 4
CAP = 80
CORES = 2
MESH = pl.DeviceIdType.MESH
VMEM_LIMIT = 60 * 1024 * 1024


def prefix(value, axis, combine, identity):
    length, mine = (lax.axis_size(axis), lax.axis_index(axis))
    everything = jax.tree.map(
        lambda part, kind: lax.all_gather(part.astype(kind), axis),
        value,
        (jnp.bfloat16, jnp.bfloat16),
    )
    start = jax.tree.map(
        lambda part, zero: jnp.broadcast_to(jnp.asarray(zero, part.dtype), part.shape),
        value,
        identity,
    )

    def hop(k, before):
        reached = k < mine
        new = combine(
            before, jax.tree.map(lambda part, own: part[k].astype(own.dtype), everything, value)
        )
        return jax.tree.map(lambda a, b: jnp.where(reached, a, b), new, before)

    return lax.fori_loop(0, length, hop, start)


def flip(value, by):
    low, high = (lax.rem(value, 2), value // 2)
    low = 1 - low if by % 2 else low
    high = 1 - high if by // 2 else high
    return low + 2 * high


def column_tile(columns):
    for tile in (512, 384, 256, 128):
        if columns % tile == 0:
            return tile
    return columns


class Place:
    def __init__(self, group):
        self.group = group
        self.height = lax.axis_size("head") // CORES
        seq, head = (lax.axis_index("seq"), lax.axis_index("head"))
        self.expert, self.x = (seq // group, lax.rem(seq, group))
        self.y, self.core = (head // CORES, lax.rem(head, CORES))
        self.head = head
        self.offsets = [
            (dx, dy) for dx in range(group) for dy in range(self.height) if (dx, dy) != (0, 0)
        ]
        self.offsets.sort(key=lambda pair: (pair[0] != 0) + (pair[1] != 0))

    def column(self, y, core):
        return y * CORES + core

    def ahead(self, dx, dy):
        return lax.rem(self.x + dx, self.group), lax.rem(self.y + dy, self.height)

    def behind(self, dx, dy):
        return (
            lax.rem(self.x + self.group - dx, self.group),
            lax.rem(self.y + self.height - dy, self.height),
        )

    def partner(self):
        return self.expert * self.group + self.x, self.column(self.y, 1 - self.core)

    def plane(self, dx, dy):
        x, y = self.ahead(dx, dy)
        return self.expert * self.group + x, self.column(y, self.core)

    def along(self, k):
        return flip(self.expert, k) * self.group + self.x, self.head

    def greet(self):
        barrier = pltpu.get_barrier_semaphore()
        targets = [self.partner()]
        targets += [self.plane(dx, dy) for dx, dy in self.offsets]
        targets += [self.along(k) for k in range(1, EXPERTS)]
        for target in targets:
            pl.semaphore_signal(barrier, inc=1, device_id=target, device_id_type=MESH)
        pl.semaphore_wait(barrier, len(targets))


def remote(source, target, send, receive, device):
    return pltpu.make_async_remote_copy(
        src_ref=source,
        dst_ref=target,
        send_sem=send,
        recv_sem=receive,
        device_id=device,
        device_id_type=MESH,
    )


def inputs_kernel(
    group,
    scale_ref,
    packed_ref,
    gate_ref,
    up_ref,
    act_ref,
    rows,
    gate_held,
    up_held,
    gate_sum,
    up_sum,
    arrived,
    sent_along,
    sent_plane,
    sent_core,
    loaded,
    local_sem,
):
    at = Place(group)
    width = packed_ref.shape[2]
    columns = gate_ref.shape[1]
    tile = column_tile(columns)
    partner = at.partner()
    count = len(at.offsets)
    order = []
    for dy in range(at.height):
        y = lax.rem(at.y + dy, at.height)
        order += [at.column(y, at.core), at.column(y, 1 - at.core)]

    loads = []
    for step, head in enumerate(order):
        part = pl.ds(pl.multiple_of(head * width, width), width)
        loads.append(
            (
                pltpu.make_async_copy(gate_ref.at[part], gate_held.at[part], loaded.at[0, step]),
                pltpu.make_async_copy(up_ref.at[part], up_held.at[part], loaded.at[1, step]),
            )
        )
        loads[-1][0].start()
        loads[-1][1].start()
    own = pltpu.make_async_copy(packed_ref.at[at.expert], rows.at[at.head, 0, at.x], local_sem)
    own.start()
    at.greet()

    started = []

    def push(source, head, k, x, send, device):
        copy = remote(source, rows.at[head, k, x], send, arrived.at[head, k, x], device)
        copy.start()
        started.append(copy)

    def landed(head, k, x):
        block = rows.at[head, k, x]
        remote(block, block, sent_along.at[0], arrived.at[head, k, x], partner).wait_recv()

    for k in (1, 2, 3):
        push(packed_ref.at[flip(at.expert, k)], at.head, k, at.x, sent_along.at[k - 1], at.along(k))
    own.wait()

    def launch(k):
        if k:
            landed(at.head, k, at.x)
        block = rows.at[at.head, k, at.x]
        for number, (dx, dy) in enumerate(at.offsets):
            push(block, at.head, k, at.x, sent_plane.at[k, number], at.plane(dx, dy))
        push(block, at.head, k, at.x, sent_core.at[k, count], partner)

    def relay(k):
        for number, (dx, dy) in enumerate(at.offsets):
            x, y = at.behind(dx, dy)
            head = at.column(y, at.core)
            landed(head, k, x)
            push(rows.at[head, k, x], head, k, x, sent_core.at[k, number], partner)

    def multiply(phase, step):
        head = order[step]
        for k in (2 * phase, 2 * phase + 1):
            if step % 2:
                for x in range(group):
                    landed(head, k, x)
        if phase == 0:
            loads[step][0].wait()
            loads[step][1].wait()
        depth = pl.ds(pl.multiple_of(head * width, width), width)

        def body(index, carry):
            if tile == columns:
                part = slice(None)
            else:
                part = pl.ds(pl.multiple_of(index * tile, tile), tile)
            block = rows[head, 2 * phase : 2 * phase + 2].reshape(gate_sum.shape[0], width)
            for held, total in ((gate_held, gate_sum), (up_held, up_sum)):
                product = jnp.dot(block, held[depth, part], preferred_element_type=jnp.float32)
                if step == 0:
                    total[:, part] = product
                else:
                    total[:, part] += product
            return carry

        lax.fori_loop(0, columns // tile, body, 0)

    def activate(phase):
        block_rows = gate_sum.shape[0] // 2
        for half in range(2):
            inner = slice(half * block_rows, (half + 1) * block_rows)
            gate = gate_sum[inner, :] * scale_ref[0]
            up = up_sum[inner, :] * scale_ref[1]
            value = gate / (1.0 + jnp.exp(-gate)) * up
            act_ref[2 * phase + half] = value.astype(jnp.bfloat16)

    launch(0)
    launch(1)
    relay(0)
    launch(2)
    relay(1)
    launch(3)
    half = len(order) // 2
    for step in range(len(order)):
        if step == half:
            relay(2)
        multiply(0, step)
    activate(0)
    relay(3)
    for step in range(len(order)):
        multiply(1, step)
    activate(1)
    for copy in started:
        copy.wait_send()


def expert_inputs(factors, packed, gate_weight, up_weight, group):
    experts, cap, width = packed.shape
    heads = lax.axis_size("head")
    depth, columns = gate_weight.shape
    others = group * heads // CORES - 1
    half = experts * group * cap // 2
    vmem = pl.BlockSpec(memory_space=pltpu.VMEM)
    return pl.pallas_call(
        functools.partial(inputs_kernel, group),
        out_shape=jax.ShapeDtypeStruct((experts, group * cap, columns), jnp.bfloat16),
        in_specs=[
            pl.BlockSpec(memory_space=pltpu.SMEM),
            vmem,
            pl.BlockSpec(memory_space=pl.ANY),
            pl.BlockSpec(memory_space=pl.ANY),
        ],
        out_specs=vmem,
        scratch_shapes=[
            pltpu.VMEM((heads, experts, group, cap, width), jnp.bfloat16),
            pltpu.VMEM((depth, columns), jnp.bfloat16),
            pltpu.VMEM((depth, columns), jnp.bfloat16),
            pltpu.VMEM((half, columns), jnp.float32),
            pltpu.VMEM((half, columns), jnp.float32),
            pltpu.SemaphoreType.DMA((heads, experts, group)),
            pltpu.SemaphoreType.DMA((experts - 1,)),
            pltpu.SemaphoreType.DMA((experts, others)),
            pltpu.SemaphoreType.DMA((experts, others + 1)),
            pltpu.SemaphoreType.DMA((2, heads)),
            pltpu.SemaphoreType.DMA,
        ],
        compiler_params=pltpu.CompilerParams(
            collective_id=1, has_side_effects=True, vmem_limit_bytes=VMEM_LIMIT
        ),
    )(factors, packed, gate_weight, up_weight)


SEND_ORDER = (2, 3, 1, 0)


def outputs_kernel(
    group,
    scale_ref,
    act_ref,
    down_ref,
    returned_ref,
    held,
    outgoing,
    incoming,
    sums,
    landing,
    finished,
    core_sent,
    core_arrived,
    plane_sent,
    plane_arrived,
    along_sent,
    along_arrived,
    loaded,
):
    at = Place(group)
    width = returned_ref.shape[2]
    cap = returned_ref.shape[1]
    tile = column_tile(width)
    partner = at.partner()
    height = at.height
    turns = list(range(height - 1, -1, -1))

    def columns_of(turn, mine):
        y = lax.rem(at.y + turn, height)
        return at.column(y, at.core if mine else 1 - at.core)

    loads = {}
    for place, turn in enumerate(turns):
        for mine in (0, 1):
            part = pl.ds(pl.multiple_of(columns_of(turn, mine) * width, width), width)
            copy = pltpu.make_async_copy(
                down_ref.at[:, part], held.at[:, part], loaded.at[place, mine]
            )
            copy.start()
            loads[turn, mine] = copy
    at.greet()
    started = []

    def product(turn, mine, target):
        loads[turn, mine].wait()
        first = columns_of(turn, mine) * width

        def body(index, carry):
            part = pl.ds(pl.multiple_of(first + index * tile, tile), tile)
            inner = pl.ds(pl.multiple_of(index * tile, tile), tile)
            for pair in range(2):
                rows = act_ref[2 * pair : 2 * pair + 2].reshape(2 * group * cap, act_ref.shape[2])
                value = jnp.dot(rows, held[:, part], preferred_element_type=jnp.float32)
                value = (value * scale_ref[0]).astype(jnp.bfloat16)
                target[turn, 2 * pair : 2 * pair + 2, :, :, inner] = value.reshape(
                    2, group, cap, tile
                )
            return carry

        lax.fori_loop(0, width // tile, body, 0)

    def core_copy(turn):
        return remote(
            outgoing.at[turn],
            incoming.at[turn],
            core_sent.at[turn],
            core_arrived.at[turn],
            partner,
        )

    def plane_copy(number, k, source, device):
        return remote(
            source,
            landing.at[number, k],
            plane_sent.at[number, k],
            plane_arrived.at[number, k],
            device,
        )

    def join(turn):
        core_copy(turn).wait_recv()
        offsets = [pair for pair in at.offsets if pair[1] == turn]
        offsets.sort(key=lambda pair: -pair[0])
        for k in SEND_ORDER:
            for x in range(group):
                sums[turn, k, x] = (
                    sums[turn, k, x].astype(jnp.float32) + incoming[turn, k, x].astype(jnp.float32)
                ).astype(jnp.bfloat16)
            for dx, dy in offsets:
                x, _ = at.ahead(dx, dy)
                copy = plane_copy(
                    at.offsets.index((dx, dy)), k, sums.at[turn, k, x], at.plane(dx, dy)
                )
                copy.start()
                started.append(copy)

    previous = None
    for turn in turns:
        product(turn, 0, outgoing)
        copy = core_copy(turn)
        copy.start()
        started.append(copy)
        if previous is not None:
            join(previous)
        product(turn, 1, sums)
        previous = turn
    join(previous)
    for k in SEND_ORDER:
        total = sums[0, k, at.x].astype(jnp.float32)
        for number, (dx, dy) in enumerate(at.offsets):
            plane_copy(number, k, landing.at[number, k], partner).wait_recv()
            total = total + landing[number, k].astype(jnp.float32)
        if k == 0:
            returned_ref[at.expert] = total.astype(jnp.bfloat16)
        else:
            finished[k - 1] = total.astype(jnp.bfloat16)
            copy = remote(
                finished.at[k - 1],
                returned_ref.at[at.expert],
                along_sent.at[k - 1],
                along_arrived.at[k - 1],
                at.along(k),
            )
            copy.start()
            started.append(copy)
    for k in (1, 2, 3):
        block = returned_ref.at[flip(at.expert, k)]
        remote(
            finished.at[k - 1], block, along_sent.at[k - 1], along_arrived.at[k - 1], at.along(k)
        ).wait_recv()
    for copy in started:
        copy.wait_send()


def expert_outputs(factor, act, down_weight, group):
    experts, cap, columns = act.shape
    cap = cap // group
    heads = lax.axis_size("head")
    depth, features = down_weight.shape
    width = features // heads
    height = heads // CORES
    others = group * height - 1
    vmem = pl.BlockSpec(memory_space=pltpu.VMEM)
    block = (height, experts, group, cap, width)
    return pl.pallas_call(
        functools.partial(outputs_kernel, group),
        out_shape=jax.ShapeDtypeStruct((experts, cap, width), jnp.bfloat16),
        in_specs=[
            pl.BlockSpec(memory_space=pltpu.SMEM),
            vmem,
            pl.BlockSpec(memory_space=pl.ANY),
        ],
        out_specs=vmem,
        scratch_shapes=[
            pltpu.VMEM((depth, features), jnp.bfloat16),
            pltpu.VMEM(block, jnp.bfloat16),
            pltpu.VMEM(block, jnp.bfloat16),
            pltpu.VMEM(block, jnp.bfloat16),
            pltpu.VMEM((others, experts, cap, width), jnp.bfloat16),
            pltpu.VMEM((experts - 1, cap, width), jnp.bfloat16),
            pltpu.SemaphoreType.DMA((height,)),
            pltpu.SemaphoreType.DMA((height,)),
            pltpu.SemaphoreType.DMA((others, experts)),
            pltpu.SemaphoreType.DMA((others, experts)),
            pltpu.SemaphoreType.DMA((experts - 1,)),
            pltpu.SemaphoreType.DMA((experts - 1,)),
            pltpu.SemaphoreType.DMA((height, 2)),
        ],
        compiler_params=pltpu.CompilerParams(
            collective_id=2, has_side_effects=True, vmem_limit_bytes=VMEM_LIMIT
        ),
    )(factor, act, down_weight)


def combine_states(earlier, later):
    return (earlier[0] * later[0], later[0][:, None, None] * earlier[1] + later[1])


def local(
    queries,
    memory_keys,
    memory_values,
    log_decay,
    hidden_in,
    out_weight,
    routes,
    route_weight,
    gate_weight,
    up_weight,
    down_weight,
    scales,
):
    tokens = queries.shape[0]
    heads = log_decay.shape[1]
    sequence_count = lax.axis_size("seq")
    group = sequence_count // EXPERTS
    token_position = lax.axis_index("seq")
    owner = token_position // group
    query_rows = queries.reshape(tokens, heads, HEAD_DIM)
    key_rows = memory_keys.reshape(tokens, heads, HEAD_DIM)
    value_rows = memory_values.reshape(tokens, heads, HEAD_DIM)
    cumulative = jnp.cumsum(log_decay, axis=0)
    total = cumulative[tokens - 1]
    scores = jnp.einsum("thd,shd->hts", query_rows, key_rows, preferred_element_type=jnp.float32)
    spread = cumulative.T[:, :, None] - cumulative.T[:, None, :]
    causal = lax.broadcasted_iota(jnp.int32, (tokens, tokens), 0) >= lax.broadcasted_iota(
        jnp.int32, (tokens, tokens), 1
    )
    weights = jnp.where(causal[None], scores * jnp.exp(jnp.minimum(spread, 0.0)), 0.0).astype(
        jnp.bfloat16
    )
    inside = jnp.einsum("hts,shd->thd", weights, value_rows, preferred_element_type=jnp.float32)
    decayed = (
        key_rows.astype(jnp.float32) * jnp.exp(total[None, :] - cumulative)[:, :, None]
    ).astype(jnp.bfloat16)
    state = jnp.einsum("shd,she->hde", decayed, value_rows, preferred_element_type=jnp.float32)
    identity = (jnp.ones_like(total), jnp.zeros_like(state))
    carried = prefix((jnp.exp(total), state), "seq", combine_states, identity)[1]
    lifted = query_rows.astype(jnp.float32) * jnp.exp(cumulative)[:, :, None]
    across = jnp.einsum("thd,hde->the", lifted, carried, precision=lax.Precision.HIGHEST)
    mixer_output = inside + across
    heads_out = (
        mixer_output
        * lax.rsqrt(jnp.mean(mixer_output * mixer_output, axis=2, keepdims=True) + 1e-06)
    ).astype(jnp.bfloat16)
    mapped_vectors = jnp.dot(
        heads_out.reshape(tokens, heads * HEAD_DIM), out_weight, preferred_element_type=jnp.float32
    )
    attention = lax.psum_scatter(
        mapped_vectors.astype(jnp.bfloat16), "head", scatter_dimension=1, tiled=True
    ).astype(jnp.float32) * (scales[1] * 0.5 * (HEADS * HEAD_DIM) ** (-0.5))
    resid = scales[0] / 64.0 * hidden_in.astype(jnp.float32) + attention
    squares = lax.psum(jnp.sum(resid * resid, axis=1), "head")
    normed = (resid * lax.rsqrt(squares[:, None] / D + 1e-05)).astype(jnp.bfloat16)
    expert_ids = lax.broadcasted_iota(jnp.int32, (tokens, EXPERTS), 1)
    hits = jnp.logical_or(routes[:, 0:1] == expert_ids, routes[:, 1:2] == expert_ids).astype(
        jnp.int32
    )
    places = jnp.cumsum(hits, axis=0, dtype=jnp.int32) - hits
    slots = lax.broadcasted_iota(jnp.int32, (EXPERTS, CAP, tokens), 1)
    picks = jnp.logical_and(places.T[:, None, :] == slots, hits.T[:, None, :] > 0)
    packed = jnp.dot(
        picks.reshape(EXPERTS * CAP, tokens).astype(jnp.bfloat16),
        normed,
        preferred_element_type=jnp.float32,
    ).astype(jnp.bfloat16)
    gate_scale = scales[2 + owner] * D ** (-0.5)
    up_scale = scales[2 + EXPERTS + owner] * D ** (-0.5)
    down_scale = scales[2 + 2 * EXPERTS + owner] * FF ** (-0.5)
    act = expert_inputs(
        jnp.stack([gate_scale, up_scale]),
        packed.reshape(EXPERTS, CAP, packed.shape[1]),
        gate_weight,
        up_weight,
        group,
    )
    returned = expert_outputs(down_scale.reshape(1), act, down_weight, group)
    flat = returned.reshape(EXPERTS * CAP, returned.shape[2])
    chosen = routes * CAP + jnp.take_along_axis(places, routes, axis=1)
    lanes = lax.broadcasted_iota(jnp.int32, (tokens, EXPERTS * CAP), 1)
    moe = 0.0
    for route in range(routes.shape[1]):
        one_hot = (chosen[:, route : route + 1] == lanes).astype(jnp.bfloat16)
        picked = jnp.dot(one_hot, flat, preferred_element_type=jnp.float32)
        moe = moe + route_weight[:, route : route + 1] * picked
    return (resid + moe).astype(jnp.bfloat16)


def solution(mesh):
    placed = (
        P("seq", "head"),
        P("seq", "head"),
        P("seq", "head"),
        P("seq", "head"),
        P("seq", "head"),
        P("head", None),
        P("seq", None),
        P("seq", None),
        P(None, ("seq", "head")),
        P(None, ("seq", "head")),
        P(("seq", "head"), None),
        P(),
    )
    return jax.shard_map(
        local, mesh=mesh, in_specs=placed, out_specs=P("seq", "head"), check_vma=False
    )
```

```python
import functools

import jax
import jax.numpy as jnp
from jax import lax
from jax.experimental import pallas as pl
from jax.experimental.pallas import tpu as pltpu
from jax.sharding import PartitionSpec as P

D = 6144
FF = 9216
HEADS = 64
HEAD_DIM = 128
EXPERTS = 4
CAP = 80
CORES = 2
MESH = pl.DeviceIdType.MESH
VMEM_LIMIT = 60 * 1024 * 1024


def carried_states(decay, state, axis):
    parts = lax.axis_size(axis)
    flat = state.astype(jnp.bfloat16).reshape(parts, -1, HEAD_DIM)
    rows = flat.shape[1]
    factors = jnp.repeat(decay, state.shape[1]).reshape(parts, rows)
    unit = 16 * HEAD_DIM
    factors = jnp.pad(factors, ((0, 0), (0, -rows % unit))).reshape(parts, -1, HEAD_DIM)
    sent = jnp.concatenate([flat, factors.astype(jnp.bfloat16)], axis=1)
    blocks = lax.all_to_all(sent, axis, split_axis=0, concat_axis=0, tiled=True)
    steps = blocks[:, :rows].astype(jnp.float32)
    fades = blocks[:, rows:].reshape(parts, -1)[:, :rows].astype(jnp.float32)
    carried, before = jnp.zeros_like(steps[0]), []
    for k in range(parts):
        before.append(carried.astype(jnp.bfloat16))
        carried = fades[k][:, None] * carried + steps[k]
    back = lax.all_to_all(jnp.stack(before), axis, split_axis=0, concat_axis=0, tiled=True)
    return back.reshape(state.shape).astype(jnp.float32)


def flip(value, by):
    low, high = (lax.rem(value, 2), value // 2)
    low = 1 - low if by % 2 else low
    high = 1 - high if by // 2 else high
    return low + 2 * high


def column_tile(columns):
    for tile in (512, 384, 256, 128):
        if columns % tile == 0:
            return tile
    return columns


class Place:
    def __init__(self, group):
        self.group = group
        self.height = lax.axis_size("head") // CORES
        seq, head = (lax.axis_index("seq"), lax.axis_index("head"))
        self.expert, self.x = (seq // group, lax.rem(seq, group))
        self.y, self.core = (head // CORES, lax.rem(head, CORES))
        self.head = head
        self.offsets = [
            (dx, dy) for dx in range(group) for dy in range(self.height) if (dx, dy) != (0, 0)
        ]
        self.offsets.sort(key=lambda pair: (pair[0] != 0) + (pair[1] != 0))

    def column(self, y, core):
        return y * CORES + core

    def ahead(self, dx, dy):
        return lax.rem(self.x + dx, self.group), lax.rem(self.y + dy, self.height)

    def behind(self, dx, dy):
        return (
            lax.rem(self.x + self.group - dx, self.group),
            lax.rem(self.y + self.height - dy, self.height),
        )

    def partner(self):
        return self.expert * self.group + self.x, self.column(self.y, 1 - self.core)

    def plane(self, dx, dy):
        x, y = self.ahead(dx, dy)
        return self.expert * self.group + x, self.column(y, self.core)

    def along(self, k):
        return flip(self.expert, k) * self.group + self.x, self.head

    def greet(self):
        barrier = pltpu.get_barrier_semaphore()
        targets = [self.partner()]
        targets += [self.plane(dx, dy) for dx, dy in self.offsets]
        targets += [self.along(k) for k in range(1, EXPERTS)]
        for target in targets:
            pl.semaphore_signal(barrier, inc=1, device_id=target, device_id_type=MESH)
        pl.semaphore_wait(barrier, len(targets))


def remote(source, target, send, receive, device):
    return pltpu.make_async_remote_copy(
        src_ref=source,
        dst_ref=target,
        send_sem=send,
        recv_sem=receive,
        device_id=device,
        device_id_type=MESH,
    )


def inputs_kernel(
    group,
    scale_ref,
    packed_ref,
    gate_ref,
    up_ref,
    act_ref,
    rows,
    gate_held,
    up_held,
    gate_sum,
    up_sum,
    arrived,
    sent_along,
    sent_plane,
    sent_core,
    loaded,
    local_sem,
):
    at = Place(group)
    width = packed_ref.shape[2]
    columns = gate_ref.shape[1]
    tile = column_tile(columns)
    partner = at.partner()
    count = len(at.offsets)
    order = []
    for dy in range(at.height):
        y = lax.rem(at.y + dy, at.height)
        order += [at.column(y, at.core), at.column(y, 1 - at.core)]

    loads = []
    for step, head in enumerate(order):
        part = pl.ds(pl.multiple_of(head * width, width), width)
        loads.append(
            (
                pltpu.make_async_copy(gate_ref.at[part], gate_held.at[part], loaded.at[0, step]),
                pltpu.make_async_copy(up_ref.at[part], up_held.at[part], loaded.at[1, step]),
            )
        )
        loads[-1][0].start()
        loads[-1][1].start()
    own = pltpu.make_async_copy(packed_ref.at[at.expert], rows.at[at.head, 0, at.x], local_sem)
    own.start()
    at.greet()

    started = []

    def push(source, head, k, x, send, device):
        copy = remote(source, rows.at[head, k, x], send, arrived.at[head, k, x], device)
        copy.start()
        started.append(copy)

    def landed(head, k, x):
        block = rows.at[head, k, x]
        remote(block, block, sent_along.at[0], arrived.at[head, k, x], partner).wait_recv()

    for k in (1, 2, 3):
        push(packed_ref.at[flip(at.expert, k)], at.head, k, at.x, sent_along.at[k - 1], at.along(k))
    own.wait()

    def launch(k):
        if k:
            landed(at.head, k, at.x)
        block = rows.at[at.head, k, at.x]
        for number, (dx, dy) in enumerate(at.offsets):
            push(block, at.head, k, at.x, sent_plane.at[k, number], at.plane(dx, dy))
        push(block, at.head, k, at.x, sent_core.at[k, count], partner)

    def relay(k):
        for number, (dx, dy) in enumerate(at.offsets):
            x, y = at.behind(dx, dy)
            head = at.column(y, at.core)
            landed(head, k, x)
            push(rows.at[head, k, x], head, k, x, sent_core.at[k, number], partner)

    def multiply(phase, step):
        head = order[step]
        for k in (2 * phase, 2 * phase + 1):
            if step % 2:
                for x in range(group):
                    landed(head, k, x)
        if phase == 0:
            loads[step][0].wait()
            loads[step][1].wait()
        depth = pl.ds(pl.multiple_of(head * width, width), width)

        def body(index, carry):
            if tile == columns:
                part = slice(None)
            else:
                part = pl.ds(pl.multiple_of(index * tile, tile), tile)
            block = rows[head, 2 * phase : 2 * phase + 2].reshape(gate_sum.shape[0], width)
            for held, total in ((gate_held, gate_sum), (up_held, up_sum)):
                product = jnp.dot(block, held[depth, part], preferred_element_type=jnp.float32)
                if step == 0:
                    total[:, part] = product
                else:
                    total[:, part] += product
            return carry

        lax.fori_loop(0, columns // tile, body, 0)

    def activate(phase):
        block_rows = gate_sum.shape[0] // 2
        for half in range(2):
            inner = slice(half * block_rows, (half + 1) * block_rows)
            gate = gate_sum[inner, :] * scale_ref[0]
            up = up_sum[inner, :] * scale_ref[1]
            value = gate / (1.0 + jnp.exp(-gate)) * up
            act_ref[2 * phase + half] = value.astype(jnp.bfloat16)

    launch(0)
    launch(1)
    relay(0)
    launch(2)
    relay(1)
    launch(3)
    half = len(order) // 2
    for step in range(len(order)):
        if step == half:
            relay(2)
        multiply(0, step)
    activate(0)
    relay(3)
    for step in range(len(order)):
        multiply(1, step)
    activate(1)
    for copy in started:
        copy.wait_send()


def expert_inputs(factors, packed, gate_weight, up_weight, group):
    experts, cap, width = packed.shape
    heads = lax.axis_size("head")
    depth, columns = gate_weight.shape
    others = group * heads // CORES - 1
    half = experts * group * cap // 2
    vmem = pl.BlockSpec(memory_space=pltpu.VMEM)
    return pl.pallas_call(
        functools.partial(inputs_kernel, group),
        out_shape=jax.ShapeDtypeStruct((experts, group * cap, columns), jnp.bfloat16),
        in_specs=[
            pl.BlockSpec(memory_space=pltpu.SMEM),
            vmem,
            pl.BlockSpec(memory_space=pl.ANY),
            pl.BlockSpec(memory_space=pl.ANY),
        ],
        out_specs=vmem,
        scratch_shapes=[
            pltpu.VMEM((heads, experts, group, cap, width), jnp.bfloat16),
            pltpu.VMEM((depth, columns), jnp.bfloat16),
            pltpu.VMEM((depth, columns), jnp.bfloat16),
            pltpu.VMEM((half, columns), jnp.float32),
            pltpu.VMEM((half, columns), jnp.float32),
            pltpu.SemaphoreType.DMA((heads, experts, group)),
            pltpu.SemaphoreType.DMA((experts - 1,)),
            pltpu.SemaphoreType.DMA((experts, others)),
            pltpu.SemaphoreType.DMA((experts, others + 1)),
            pltpu.SemaphoreType.DMA((2, heads)),
            pltpu.SemaphoreType.DMA,
        ],
        compiler_params=pltpu.CompilerParams(
            collective_id=1, has_side_effects=True, vmem_limit_bytes=VMEM_LIMIT
        ),
    )(factors, packed, gate_weight, up_weight)


SEND_ORDER = (2, 3, 1, 0)


def outputs_kernel(
    group,
    scale_ref,
    act_ref,
    down_ref,
    returned_ref,
    held,
    outgoing,
    incoming,
    sums,
    landing,
    finished,
    core_sent,
    core_arrived,
    plane_sent,
    plane_arrived,
    along_sent,
    along_arrived,
    loaded,
):
    at = Place(group)
    width = returned_ref.shape[2]
    cap = returned_ref.shape[1]
    tile = column_tile(width)
    partner = at.partner()
    height = at.height
    turns = list(range(height - 1, -1, -1))

    def columns_of(turn, mine):
        y = lax.rem(at.y + turn, height)
        return at.column(y, at.core if mine else 1 - at.core)

    loads = {}
    for place, turn in enumerate(turns):
        for mine in (0, 1):
            part = pl.ds(pl.multiple_of(columns_of(turn, mine) * width, width), width)
            copy = pltpu.make_async_copy(
                down_ref.at[:, part], held.at[:, part], loaded.at[place, mine]
            )
            copy.start()
            loads[turn, mine] = copy
    at.greet()
    started = []

    def product(turn, mine, target):
        loads[turn, mine].wait()
        first = columns_of(turn, mine) * width

        def body(index, carry):
            part = pl.ds(pl.multiple_of(first + index * tile, tile), tile)
            inner = pl.ds(pl.multiple_of(index * tile, tile), tile)
            for pair in range(2):
                rows = act_ref[2 * pair : 2 * pair + 2].reshape(2 * group * cap, act_ref.shape[2])
                value = jnp.dot(rows, held[:, part], preferred_element_type=jnp.float32)
                value = (value * scale_ref[0]).astype(jnp.bfloat16)
                target[turn, 2 * pair : 2 * pair + 2, :, :, inner] = value.reshape(
                    2, group, cap, tile
                )
            return carry

        lax.fori_loop(0, width // tile, body, 0)

    def core_copy(turn):
        return remote(
            outgoing.at[turn],
            incoming.at[turn],
            core_sent.at[turn],
            core_arrived.at[turn],
            partner,
        )

    def plane_copy(number, k, source, device):
        return remote(
            source,
            landing.at[number, k],
            plane_sent.at[number, k],
            plane_arrived.at[number, k],
            device,
        )

    def join(turn):
        core_copy(turn).wait_recv()
        offsets = [pair for pair in at.offsets if pair[1] == turn]
        offsets.sort(key=lambda pair: -pair[0])
        for k in SEND_ORDER:
            for x in range(group):
                sums[turn, k, x] = (
                    sums[turn, k, x].astype(jnp.float32) + incoming[turn, k, x].astype(jnp.float32)
                ).astype(jnp.bfloat16)
            for dx, dy in offsets:
                x, _ = at.ahead(dx, dy)
                copy = plane_copy(
                    at.offsets.index((dx, dy)), k, sums.at[turn, k, x], at.plane(dx, dy)
                )
                copy.start()
                started.append(copy)

    previous = None
    for turn in turns:
        product(turn, 0, outgoing)
        copy = core_copy(turn)
        copy.start()
        started.append(copy)
        if previous is not None:
            join(previous)
        product(turn, 1, sums)
        previous = turn
    join(previous)
    for k in SEND_ORDER:
        total = sums[0, k, at.x].astype(jnp.float32)
        for number, (dx, dy) in enumerate(at.offsets):
            plane_copy(number, k, landing.at[number, k], partner).wait_recv()
            total = total + landing[number, k].astype(jnp.float32)
        if k == 0:
            returned_ref[at.expert] = total.astype(jnp.bfloat16)
        else:
            finished[k - 1] = total.astype(jnp.bfloat16)
            copy = remote(
                finished.at[k - 1],
                returned_ref.at[at.expert],
                along_sent.at[k - 1],
                along_arrived.at[k - 1],
                at.along(k),
            )
            copy.start()
            started.append(copy)
    for k in (1, 2, 3):
        block = returned_ref.at[flip(at.expert, k)]
        remote(
            finished.at[k - 1], block, along_sent.at[k - 1], along_arrived.at[k - 1], at.along(k)
        ).wait_recv()
    for copy in started:
        copy.wait_send()


def expert_outputs(factor, act, down_weight, group):
    experts, cap, columns = act.shape
    cap = cap // group
    heads = lax.axis_size("head")
    depth, features = down_weight.shape
    width = features // heads
    height = heads // CORES
    others = group * height - 1
    vmem = pl.BlockSpec(memory_space=pltpu.VMEM)
    block = (height, experts, group, cap, width)
    return pl.pallas_call(
        functools.partial(outputs_kernel, group),
        out_shape=jax.ShapeDtypeStruct((experts, cap, width), jnp.bfloat16),
        in_specs=[
            pl.BlockSpec(memory_space=pltpu.SMEM),
            vmem,
            pl.BlockSpec(memory_space=pl.ANY),
        ],
        out_specs=vmem,
        scratch_shapes=[
            pltpu.VMEM((depth, features), jnp.bfloat16),
            pltpu.VMEM(block, jnp.bfloat16),
            pltpu.VMEM(block, jnp.bfloat16),
            pltpu.VMEM(block, jnp.bfloat16),
            pltpu.VMEM((others, experts, cap, width), jnp.bfloat16),
            pltpu.VMEM((experts - 1, cap, width), jnp.bfloat16),
            pltpu.SemaphoreType.DMA((height,)),
            pltpu.SemaphoreType.DMA((height,)),
            pltpu.SemaphoreType.DMA((others, experts)),
            pltpu.SemaphoreType.DMA((others, experts)),
            pltpu.SemaphoreType.DMA((experts - 1,)),
            pltpu.SemaphoreType.DMA((experts - 1,)),
            pltpu.SemaphoreType.DMA((height, 2)),
        ],
        compiler_params=pltpu.CompilerParams(
            collective_id=2, has_side_effects=True, vmem_limit_bytes=VMEM_LIMIT
        ),
    )(factor, act, down_weight)


def local(
    queries,
    memory_keys,
    memory_values,
    log_decay,
    hidden_in,
    out_weight,
    routes,
    route_weight,
    gate_weight,
    up_weight,
    down_weight,
    scales,
):
    tokens = queries.shape[0]
    heads = log_decay.shape[1]
    sequence_count = lax.axis_size("seq")
    group = sequence_count // EXPERTS
    token_position = lax.axis_index("seq")
    owner = token_position // group
    query_rows = queries.reshape(tokens, heads, HEAD_DIM)
    key_rows = memory_keys.reshape(tokens, heads, HEAD_DIM)
    value_rows = memory_values.reshape(tokens, heads, HEAD_DIM)
    cumulative = jnp.cumsum(log_decay, axis=0)
    total = cumulative[tokens - 1]
    scores = jnp.einsum("thd,shd->hts", query_rows, key_rows, preferred_element_type=jnp.float32)
    spread = cumulative.T[:, :, None] - cumulative.T[:, None, :]
    causal = lax.broadcasted_iota(jnp.int32, (tokens, tokens), 0) >= lax.broadcasted_iota(
        jnp.int32, (tokens, tokens), 1
    )
    weights = jnp.where(causal[None], scores * jnp.exp(jnp.minimum(spread, 0.0)), 0.0).astype(
        jnp.bfloat16
    )
    inside = jnp.einsum("hts,shd->thd", weights, value_rows, preferred_element_type=jnp.float32)
    decayed = (
        key_rows.astype(jnp.float32) * jnp.exp(total[None, :] - cumulative)[:, :, None]
    ).astype(jnp.bfloat16)
    state = jnp.einsum("shd,she->hde", decayed, value_rows, preferred_element_type=jnp.float32)
    carried = carried_states(jnp.exp(total), state, "seq")
    lifted = query_rows.astype(jnp.float32) * jnp.exp(cumulative)[:, :, None]
    across = jnp.einsum("thd,hde->the", lifted, carried, precision=lax.Precision.HIGHEST)
    mixer_output = inside + across
    heads_out = (
        mixer_output
        * lax.rsqrt(jnp.mean(mixer_output * mixer_output, axis=2, keepdims=True) + 1e-06)
    ).astype(jnp.bfloat16)
    mapped_vectors = jnp.dot(
        heads_out.reshape(tokens, heads * HEAD_DIM), out_weight, preferred_element_type=jnp.float32
    )
    attention = lax.psum_scatter(
        mapped_vectors.astype(jnp.bfloat16), "head", scatter_dimension=1, tiled=True
    ).astype(jnp.float32) * (scales[1] * 0.5 * (HEADS * HEAD_DIM) ** (-0.5))
    resid = scales[0] / 64.0 * hidden_in.astype(jnp.float32) + attention
    squares = lax.psum(jnp.sum(resid * resid, axis=1), "head")
    normed = (resid * lax.rsqrt(squares[:, None] / D + 1e-05)).astype(jnp.bfloat16)
    expert_ids = lax.broadcasted_iota(jnp.int32, (tokens, EXPERTS), 1)
    hits = jnp.logical_or(routes[:, 0:1] == expert_ids, routes[:, 1:2] == expert_ids).astype(
        jnp.int32
    )
    places = jnp.cumsum(hits, axis=0, dtype=jnp.int32) - hits
    slots = lax.broadcasted_iota(jnp.int32, (EXPERTS, CAP, tokens), 1)
    picks = jnp.logical_and(places.T[:, None, :] == slots, hits.T[:, None, :] > 0)
    packed = jnp.dot(
        picks.reshape(EXPERTS * CAP, tokens).astype(jnp.bfloat16),
        normed,
        preferred_element_type=jnp.float32,
    ).astype(jnp.bfloat16)
    gate_scale = scales[2 + owner] * D ** (-0.5)
    up_scale = scales[2 + EXPERTS + owner] * D ** (-0.5)
    down_scale = scales[2 + 2 * EXPERTS + owner] * FF ** (-0.5)
    act = expert_inputs(
        jnp.stack([gate_scale, up_scale]),
        packed.reshape(EXPERTS, CAP, packed.shape[1]),
        gate_weight,
        up_weight,
        group,
    )
    returned = expert_outputs(down_scale.reshape(1), act, down_weight, group)
    flat = returned.reshape(EXPERTS * CAP, returned.shape[2])
    chosen = routes * CAP + jnp.take_along_axis(places, routes, axis=1)
    lanes = lax.broadcasted_iota(jnp.int32, (tokens, EXPERTS * CAP), 1)
    moe = 0.0
    for route in range(routes.shape[1]):
        one_hot = (chosen[:, route : route + 1] == lanes).astype(jnp.bfloat16)
        picked = jnp.dot(one_hot, flat, preferred_element_type=jnp.float32)
        moe = moe + route_weight[:, route : route + 1] * picked
    return (resid + moe).astype(jnp.bfloat16)


def solution(mesh):
    placed = (
        P("seq", "head"),
        P("seq", "head"),
        P("seq", "head"),
        P("seq", "head"),
        P("seq", "head"),
        P("head", None),
        P("seq", None),
        P("seq", None),
        P(None, ("seq", "head")),
        P(None, ("seq", "head")),
        P(("seq", "head"), None),
        P(),
    )
    return jax.shard_map(
        local, mesh=mesh, in_specs=placed, out_specs=P("seq", "head"), check_vma=False
    )
```
